32 devices in a mesh: groups: 2 (over x), sample: 8 (over z, y), feature: 2 (over core).
Axes of the slice: x: 2, y: 2, z: 4, core: 2. Of those that a mesh axis runs over, the one named last changes fastest.
Arguments:
- blk_values: bfloat16 [16, 2, 320, 128, 128], P(('groups', 'sample'), 'feature'), parts along dimension 0, may hold values from -6 to 6
- blk_rows: int32 [16, 2, 320], P(('groups', 'sample'), 'feature'), parts along dimension 0, may hold values from 0 to 31
- blk_cols: int32 [16, 2, 320], P(('groups', 'sample'), 'feature'), parts along dimension 0, may hold values from 0 to 1023, as said below
- blk_count: int32 [16, 2], P(('groups', 'sample'), 'feature'), parts along dimension 0, may hold values from 1 to 320, as said below
- boot_counts: int32 [65536, 32], P(('groups', 'sample')), parts along dimension 0, may hold values from 0 to 8, as said below
- labels: int32 [65536], P(('groups', 'sample')), parts along dimension 0, may hold values 0 or 1
- coefs: float32 [524288, 32], P(('groups', 'feature', 'sample')), parts along dimension 0, may hold values from -0.18 to 0.18
Outputs:
- gradient: float32 [524288, 32], P(('groups', 'feature', 'sample')), parts along dimension 0
The draws below stay inside these ranges and needn't reach their ends.
There are 2 independent parts, one for each index of `groups`. The reference program is written for one: setup_inputs(seed, part) draws one part's arguments, and reference() takes and returns one part's arrays. A program takes and returns all parts, laid end to end along the dimension named above; each array names one. Nothing has to cross between parts.
Inputs may be any that keep to these rules, and one draw needn't show every extreme that they name: `blk_cols`: of all 320 slots of one device, at most 40 name column blocks within one index of sample's share of the columns (the share of index k is blocks k * 262144 / (2 * 8 * 128) onward); every device reaches 40. `blk_count`: slots at or beyond a device's count hold no part of the design; some device has all 320 slots live. `boot_counts`: some entry reaches the most.
All inputs are finite; a program needn't handle non-finite values. No bound on the sum of `labels` on one device may be relied on, other than what follows from the above.
Results may differ from the reference program's by a relative error of at most 0.0031.
Values may be sent and summed in bfloat16 or wider, within the bound.
A program may use at most 128 MiB of HBM per device.

```python
import jax
import jax.numpy as jnp
from jax import lax

NF = 262144
R = 32
BLK = 128
RB = 32
BD = 320
ROWS = 32768
N_SAMPLE = 8
N_FEATURE = 2


def draw_blk_rows(key, part):
    key = jax.random.fold_in(key, 11)
    first, second = jax.random.split(key)
    upper = jax.random.randint(first, (N_SAMPLE, N_FEATURE, BD), 0, RB)
    lower = jax.random.randint(second, (N_SAMPLE, N_FEATURE, BD), 0, RB)
    return (upper * lower // max(RB - 1, 1)).astype(jnp.int32)


def draw_blk_cols(key, part):
    key = jax.random.fold_in(key, 12)
    first, second = jax.random.split(key)
    per_owner = NF // (N_FEATURE * BLK * N_SAMPLE)
    shifts = jax.random.randint(first, (N_SAMPLE, N_FEATURE, 1), 0, N_SAMPLE)
    slot_ids = jnp.arange(BD, dtype=jnp.int32)[None, None, :]
    owners = (slot_ids + shifts) % N_SAMPLE
    offsets = jax.random.randint(second, (N_SAMPLE, N_FEATURE, BD), 0, per_owner)
    return (owners * per_owner + offsets).astype(jnp.int32)


def draw_blk_count(key, part):
    key = jax.random.fold_in(key, 13)
    first, second = jax.random.split(key)
    counts = jax.random.randint(first, (N_SAMPLE * N_FEATURE,), max(BD // 4, 1), BD + 1)
    full = jax.random.randint(second, (), 0, N_SAMPLE * N_FEATURE)
    counts = jnp.where(jnp.arange(N_SAMPLE * N_FEATURE) == full, BD, counts)
    return counts.reshape(N_SAMPLE, N_FEATURE).astype(jnp.int32)


def draw_boot_counts(key, part):
    key = jax.random.fold_in(key, 14)
    first, second = jax.random.split(key)
    trials = jax.random.randint(first, (8, ROWS, R), 0, 8)
    counts = jnp.sum((trials == 0).astype(jnp.int32), axis=0).reshape(ROWS * R)
    top = jax.random.randint(second, (), 0, ROWS * R)
    counts = jnp.where(jnp.arange(ROWS * R) == top, 8, counts)
    return counts.reshape(ROWS, R).astype(jnp.int32)


def plant(array, key, least, top_value):
    extent = array.shape
    index_at = [jax.random.randint(jax.random.fold_in(key, axis), (), 0, extent[axis]) for axis in range(len(extent))]
    array = array.at[tuple(index_at)].set(least)
    longest = extent.index(max(extent))
    index_at[longest] = (index_at[longest] + 1) % extent[longest]
    return array.at[tuple(index_at)].set(top_value)


def level_of(rng, shape, shards, low, high):
    level, own = 1.0, jax.random.fold_in(rng, 6)
    for position, parts in shards:
        heights = jnp.exp(jax.random.uniform(jax.random.fold_in(own, position), (parts,), jnp.float32, low / len(shards), high / len(shards)))
        level = level * jnp.repeat(heights, shape[position] // parts).reshape([-1 if axis == position else 1 for axis in range(len(shape))])
    return level


def scatter_about(own_key, shape, spread, most, cuts=(), kind=jnp.bfloat16):
    gain = level_of(own_key, shape, cuts, -0.22, 0.18) if cuts else 1.0
    drawn = jax.random.normal(own_key, shape, jnp.float32) * spread * gain
    return jnp.minimum(jnp.maximum(drawn, -most), most).astype(kind)


def setup_inputs(seed: int = 0, part: int = 0) -> dict:
    arg_keys = jax.random.split(jax.random.key(seed), 8)
    part_splits = jax.random.split(jax.random.fold_in(arg_keys[7], part), 8)
    return {
        "blk_values": scatter_about(part_splits[0], (N_SAMPLE, N_FEATURE, BD, BLK, BLK), 1.0, 6.0, ((0, 8), (1, 2))),
        "blk_rows": draw_blk_rows(jax.random.fold_in(jax.random.fold_in(arg_keys[7], part), 71), part),
        "blk_cols": draw_blk_cols(jax.random.fold_in(jax.random.fold_in(arg_keys[7], part), 71), part),
        "blk_count": draw_blk_count(jax.random.fold_in(jax.random.fold_in(arg_keys[7], part), 71), part),
        "boot_counts": draw_boot_counts(jax.random.fold_in(jax.random.fold_in(arg_keys[7], part), 71), part),
        "labels": plant((jax.random.randint(part_splits[5], (ROWS,), 0, 2) < 1).astype(jnp.int32), jax.random.fold_in(part_splits[5], 1), 0, 1),
        "coefs": scatter_about(part_splits[6], (NF, R), 0.03, 0.18, ((0, 16),), jnp.float32),
    }


def reference(blk_values, blk_rows, blk_cols, blk_count, boot_counts, labels, coefs):
    half_blocks = NF // (N_FEATURE * BLK)
    coef_low = coefs.astype(jnp.bfloat16).reshape(N_FEATURE, half_blocks, BLK, R)
    slot_ids = jnp.arange(BD, dtype=jnp.int32)
    live = (slot_ids[None, None, :] < blk_count[:, :, None]).astype(jnp.float32)
    feat_ids = jnp.arange(N_FEATURE, dtype=jnp.int32)[:, None]

    def margins_of(s):
        values = blk_values[s].astype(jnp.float32)
        picked = coef_low[feat_ids, blk_cols[s]].astype(jnp.float32)
        prod = jnp.einsum('fbij,fbjr->fbir', values, picked) * live[s][:, :, None, None]
        return jax.ops.segment_sum(prod.reshape(N_FEATURE * BD, BLK, R), blk_rows[s].reshape(-1), num_segments=RB)

    margins = lax.map(margins_of, jnp.arange(N_SAMPLE, dtype=jnp.int32)).reshape(ROWS, R)
    counts = boot_counts.astype(jnp.float32)
    resid = (counts * (jax.nn.sigmoid(margins) - labels.astype(jnp.float32)[:, None])).astype(jnp.bfloat16)
    resid = resid.reshape(N_SAMPLE, RB, BLK, R)

    def add_slab(total, s):
        values = blk_values[s].astype(jnp.float32)
        picked = resid[s][blk_rows[s]].astype(jnp.float32)
        back = jnp.einsum('fbij,fbir->fbjr', values, picked) * live[s][:, :, None, None]
        return total.at[feat_ids, blk_cols[s]].add(back), None

    start = jnp.zeros((N_FEATURE, half_blocks, BLK, R), jnp.float32)
    total, _ = lax.scan(add_slab, start, jnp.arange(N_SAMPLE, dtype=jnp.int32))
    return total.reshape(NF, R) / 16.0
```

```python
import functools

import jax
import jax.numpy as jnp
from jax import lax
from jax.experimental import pallas as pl
from jax.experimental.pallas import tpu as pltpu
from jax.sharding import PartitionSpec as P

MESH = pl.DeviceIdType.MESH
F32 = jnp.float32
BF16 = jnp.bfloat16


def _sizes(n, slots, row_blocks):
    quota = slots // n
    step = max(u for u in range(1, 11) if quota % u == 0)
    return quota, step


def _distance(n, i):
    half = (i + 1) // 2
    return n // 2 + (1 - 2 * (i % 2)) * half


def exchange_kernel(
    n,
    quota,
    step,
    row_blocks,
    meta,
    req_ref,
    coef_ref,
    counts_ref,
    labels_ref,
    values_ref,
    asked_ref,
    grad_ref,
    vbuf,
    blocks,
    send,
    recv,
    prod,
    run,
    marg,
    marg_other,
    resid,
    gsend,
    wanted,
    v_sem,
    req_send,
    req_recv,
    want_sem,
    c_send,
    c_recv,
    m_send,
    m_recv,
    g_send,
    g_recv,
    own_sem,
):
    me = lax.axis_index("sample")
    feat = lax.axis_index("feature")
    other = 1 - feat
    width = blocks.shape[2]
    slots = n * quota

    load_values = pltpu.make_async_copy(values_ref, vbuf, v_sem)
    load_values.start()

    barrier = pltpu.get_barrier_semaphore()
    for d in range(1, n):
        pl.semaphore_signal(
            barrier, inc=1, device_id={"sample": lax.rem(me + d, n)}, device_id_type=MESH
        )
    pl.semaphore_signal(barrier, inc=1, device_id={"feature": other}, device_id_type=MESH)
    pl.semaphore_wait(barrier, n)

    def req_copy(d):
        dst = lax.rem(me + d, n)
        return pltpu.make_async_remote_copy(
            src_ref=req_ref.at[dst],
            dst_ref=asked_ref.at[me],
            send_sem=req_send.at[d],
            recv_sem=req_recv.at[d],
            device_id={"sample": dst},
            device_id_type=MESH,
        )

    def coef_copy(d):
        dst = lax.rem(me + d, n)
        return pltpu.make_async_remote_copy(
            src_ref=send.at[dst],
            dst_ref=recv.at[me],
            send_sem=c_send.at[d],
            recv_sem=c_recv.at[d],
            device_id={"sample": dst},
            device_id_type=MESH,
        )

    def grad_copy(d):
        dst = lax.rem(me + d, n)
        return pltpu.make_async_remote_copy(
            src_ref=gsend.at[dst],
            dst_ref=grad_ref.at[me],
            send_sem=g_send.at[d],
            recv_sem=g_recv.at[d],
            device_id={"sample": dst},
            device_id_type=MESH,
        )

    for i in range(n - 1):
        req_copy(_distance(n, i)).start()

    asked_ref[me] = req_ref[me]
    for b in range(blocks.shape[0]):
        blocks[b] = coef_ref[:, b * width : (b + 1) * width].astype(BF16)

    def pack(source, target, src_slot, dst_slot):
        def some(g, carry):
            for u in range(step):
                j = g * step + u
                target[dst_slot, j] = blocks[wanted[src_slot, 0, j]]
            return carry

        lax.fori_loop(0, quota // step, some, 0)

    def serve(i, carry):
        d = n - _distance(n, i)
        dst = lax.rem(me + n - d, n)
        req_copy(d).wait_recv()
        bring = pltpu.make_async_copy(asked_ref.at[dst], wanted.at[dst], want_sem)
        bring.start()
        bring.wait()
        pack(wanted, send, dst, dst)
        coef_copy(n - d).start()
        return carry

    lax.fori_loop(0, n - 1, serve, 0)

    bring = pltpu.make_async_copy(asked_ref.at[me], wanted.at[me], want_sem)
    bring.start()
    bring.wait()
    pack(wanted, recv, me, me)
    load_values.wait()

    def forward(src):
        def some(g, carry):
            for u in range(step):
                j = g * step + u
                p = src * quota + j
                prod[p] = lax.dot_general(
                    recv[src, j],
                    vbuf[meta[0, p]],
                    (((1,), (1,)), ((), ())),
                    preferred_element_type=F32,
                )
            return carry

        lax.fori_loop(0, quota // step, some, 0)

    forward(me)

    def arrive(i, carry):
        d = _distance(n, i)
        coef_copy(d).wait_recv()
        forward(lax.rem(me + n - d, n))
        return carry

    lax.fori_loop(0, n - 1, arrive, 0)

    def rowsum(g, acc):
        for u in range(step):
            q = g * step + u
            acc = acc * meta[4, q].astype(F32) + prod[meta[3, q]]
            run[q] = acc
        return acc

    lax.fori_loop(0, slots // step, rowsum, jnp.zeros(marg.shape[1:], F32))

    def take(r, carry):
        marg[r] = run[meta[5, r]] * meta[6, r].astype(F32)
        return carry

    lax.fori_loop(0, row_blocks, take, 0)

    swap = pltpu.make_async_remote_copy(
        src_ref=marg,
        dst_ref=marg_other,
        send_sem=m_send,
        recv_sem=m_recv,
        device_id={"feature": other},
        device_id_type=MESH,
    )
    swap.start()
    swap.wait()

    def residual(r, carry):
        m = marg[r] + marg_other[r]
        at = pl.ds(pl.multiple_of(r * width, width), width)
        c = counts_ref[:, at].astype(F32)
        y = labels_ref[r].astype(F32)
        resid[r] = (c * (jax.nn.sigmoid(m) - y)).astype(BF16)
        return carry

    lax.fori_loop(0, row_blocks, residual, 0)

    def backward(dst):
        def some(g, carry):
            for u in range(step):
                j = g * step + u
                p = dst * quota + j
                back = lax.dot_general(
                    resid[meta[1, p]],
                    vbuf[meta[0, p]],
                    (((1,), (0,)), ((), ())),
                    preferred_element_type=F32,
                )
                gsend[dst, j] = (back * meta[2, p].astype(F32)).astype(BF16)
            return carry

        lax.fori_loop(0, quota // step, some, 0)

    def give(i, carry):
        d = _distance(n, i)
        backward(lax.rem(me + d, n))
        grad_copy(d).start()
        return carry

    lax.fori_loop(0, n - 1, give, 0)
    backward(me)
    keep = pltpu.make_async_copy(gsend.at[me], grad_ref.at[me], own_sem)
    keep.start()

    def finish(i, carry):
        d = _distance(n, i)
        req_copy(d).wait_send()
        coef_copy(d).wait_send()
        grad_copy(d).wait_send()
        grad_copy(d).wait_recv()
        return carry

    lax.fori_loop(0, n - 1, finish, 0)
    keep.wait()


def add_kernel(n, quota, step, scale, asked, grad_ref, out_ref):
    out_ref[...] = jnp.zeros_like(out_ref)
    width = grad_ref.shape[3]

    def source(s, carry):
        def some(g, inner):
            for u in range(step):
                j = g * step + u
                at = pl.ds(pl.multiple_of(asked[s, 0, j] * width, width), width)
                out_ref[:, at] += grad_ref[s, j].astype(F32) * scale
            return inner

        return lax.fori_loop(0, quota // step, some, carry)

    lax.fori_loop(0, n, source, 0)


def plan(rows, cols, count, n, quota, share, row_blocks):
    slots = rows.shape[0]
    ids = jnp.arange(slots, dtype=jnp.int32)
    owner = cols // share
    before = ids[None, :] < ids[:, None]
    same = (owner[:, None] == owner[None, :]) & before
    rank = owner * quota + jnp.sum(same.astype(jnp.int32), axis=1)
    live = (ids < count).astype(jnp.int32)
    key = jnp.where(ids < count, rows, row_blocks)
    ahead = (key[None, :] < key[:, None]) | ((key[None, :] == key[:, None]) & before)
    row_rank = jnp.sum(ahead.astype(jnp.int32), axis=1)
    code = ((cols % share) * 2 + live) * row_blocks + rows
    code = code * slots + ids
    by_owner = jnp.sum(jnp.where(rank[None, :] == ids[:, None], code[None, :], 0), axis=1)
    row_code = key * slots + rank
    by_row = jnp.sum(jnp.where(row_rank[None, :] == ids[:, None], row_code[None, :], 0), axis=1)
    order = by_owner % slots
    rest = by_owner // slots
    row_at = rest % row_blocks
    rest = rest // row_blocks
    live_at = rest % 2
    local_col = rest // 2
    row_order = by_row % slots
    key_at = by_row // slots
    keep = (key_at == jnp.roll(key_at, 1)).astype(jnp.int32)
    blocks = jnp.arange(slots, dtype=jnp.int32)
    upto = jnp.sum((key[None, :] <= blocks[:, None]).astype(jnp.int32), axis=1)
    here = jnp.sum((key[None, :] == blocks[:, None]).astype(jnp.int32), axis=1)
    last = jnp.maximum(upto - 1, 0)
    some = (here > 0).astype(jnp.int32)
    meta = jnp.stack([order, row_at, live_at, row_order, keep, last, some, keep])
    req = jnp.zeros((n, 8, 128), jnp.int32).at[:, :, :quota].set(
        local_col.reshape(n, 1, quota)
    )
    return meta, req


def local(blk_values, blk_rows, blk_cols, blk_count, boot_counts, labels, coefs):
    values = blk_values[0, 0]
    slots, width = values.shape[0], values.shape[1]
    reps = coefs.shape[1]
    n = lax.axis_size("sample")
    row_blocks = boot_counts.shape[0] // width
    share = coefs.shape[0] // width
    quota, step = _sizes(n, slots, row_blocks)
    meta, req = plan(
        blk_rows[0, 0], blk_cols[0, 0], blk_count[0, 0], n, quota, share, row_blocks
    )
    vmem = pl.BlockSpec(memory_space=pltpu.VMEM)
    smem = pl.BlockSpec(memory_space=pltpu.SMEM)
    hbm = pl.BlockSpec(memory_space=pl.ANY)
    asked, grads = pl.pallas_call(
        functools.partial(exchange_kernel, n, quota, step, row_blocks),
        out_shape=[
            jax.ShapeDtypeStruct((n, 8, 128), jnp.int32),
            jax.ShapeDtypeStruct((n, quota, reps, width), BF16),
        ],
        in_specs=[smem, vmem, vmem, vmem, vmem, hbm],
        out_specs=[vmem, hbm],
        scratch_shapes=[
            pltpu.VMEM((slots, width, width), BF16),
            pltpu.VMEM((share, reps, width), BF16),
            pltpu.VMEM((n, quota, reps, width), BF16),
            pltpu.VMEM((n, quota, reps, width), BF16),
            pltpu.VMEM((slots, reps, width), F32),
            pltpu.VMEM((slots, reps, width), F32),
            pltpu.VMEM((row_blocks, reps, width), F32),
            pltpu.VMEM((row_blocks, reps, width), F32),
            pltpu.VMEM((row_blocks, reps, width), BF16),
            pltpu.VMEM((n, quota, reps, width), BF16),
            pltpu.SMEM((n, 8, 128), jnp.int32),
            pltpu.SemaphoreType.DMA,
            pltpu.SemaphoreType.DMA((n,)),
            pltpu.SemaphoreType.DMA((n,)),
            pltpu.SemaphoreType.DMA,
            pltpu.SemaphoreType.DMA((n,)),
            pltpu.SemaphoreType.DMA((n,)),
            pltpu.SemaphoreType.DMA,
            pltpu.SemaphoreType.DMA,
            pltpu.SemaphoreType.DMA((n,)),
            pltpu.SemaphoreType.DMA((n,)),
            pltpu.SemaphoreType.DMA,
        ],
        compiler_params=pltpu.CompilerParams(
            collective_id=0, has_side_effects=True, vmem_limit_bytes=56 * 2**20
        ),
        name="exchange",
    )(meta, req, coefs.T, boot_counts.T, labels.reshape(row_blocks, 1, width), values)
    total = pl.pallas_call(
        functools.partial(add_kernel, n, quota, step, 1.0 / 16.0),
        out_shape=jax.ShapeDtypeStruct((reps, coefs.shape[0]), F32),
        in_specs=[smem, vmem],
        out_specs=vmem,
        compiler_params=pltpu.CompilerParams(vmem_limit_bytes=32 * 2**20),
        name="add",
    )(asked, grads)
    return total.T


def solution(mesh):
    return jax.shard_map(
        local,
        mesh=mesh,
        in_specs=(
            P(("groups", "sample"), "feature", None, None, None),
            P(("groups", "sample"), "feature", None),
            P(("groups", "sample"), "feature", None),
            P(("groups", "sample"), "feature"),
            P(("groups", "sample"), None),
            P(("groups", "sample")),
            P(("groups", "feature", "sample"), None),
        ),
        out_specs=P(("groups", "feature", "sample"), None),
        check_vma=False,
    )
```

```python
import functools

import jax
import jax.numpy as jnp
from jax import lax
from jax.experimental import pallas as pl
from jax.experimental.pallas import tpu as pltpu
from jax.sharding import PartitionSpec as P

MESH = pl.DeviceIdType.MESH
F32 = jnp.float32
BF16 = jnp.bfloat16


PARTS = 2


def _sizes(n, slots):
    quota = slots // n
    step = max(u for u in range(1, 11) if quota % u == 0)
    return quota, step


def _distance(n, i):
    half = (i + 1) // 2
    return n // 2 + (1 - 2 * (i % 2)) * half


def _bits(size):
    return (size - 1).bit_length()


def exchange_kernel(
    n,
    quota,
    step,
    row_blocks,
    count_ref,
    rows_ref,
    cols_ref,
    coef_ref,
    counts_ref,
    labels_ref,
    values_ref,
    asked_out,
    grad_ref,
    vbuf,
    blocks,
    send,
    recv,
    prod,
    run,
    marg,
    marg_other,
    resid,
    gsend,
    plan,
    asked,
    sums,
    wanted,
    mine,
    meta,
    v_sem,
    req_send,
    req_recv,
    want_sem,
    asked_sem,
    c_send,
    c_recv,
    m_send,
    m_recv,
    g_send,
    g_recv,
    own_sem,
):
    me = lax.axis_index("sample")
    feat = lax.axis_index("feature")
    other = 1 - feat
    share, reps, width = blocks.shape[1:]
    slots = n * quota
    i32 = jnp.int32

    load_values = pltpu.make_async_copy(values_ref, vbuf, v_sem)
    load_values.start()

    barrier = pltpu.get_barrier_semaphore()
    for d in range(1, n):
        pl.semaphore_signal(
            barrier, inc=1, device_id={"sample": lax.rem(me + d, n)}, device_id_type=MESH
        )
    pl.semaphore_signal(barrier, inc=1, device_id={"feature": other}, device_id_type=MESH)

    ii = lax.broadcasted_iota(i32, (slots, slots), 0)
    jj = lax.broadcasted_iota(i32, (slots, slots), 1)

    def upright(row):
        return jnp.sum(jnp.where(ii == jj, row, 0), axis=1, keepdims=True)

    share_bits, row_bits, slot_bits = _bits(share), _bits(row_blocks), _bits(slots)
    cols = cols_ref[...]
    rows = rows_ref[...]
    ids = lax.broadcasted_iota(i32, (1, slots), 1)
    live = (ids < count_ref[0, 0]).astype(i32)
    owner = lax.shift_right_logical(cols, jnp.full_like(cols, share_bits))
    owner_up = upright(owner)
    same = jnp.where((owner_up == owner) & (jj < ii), 1, 0)
    rank = owner_up * quota + jnp.sum(same, axis=1, keepdims=True)
    code = (cols & (share - 1)) * 2 + live
    code = (code * (1 << row_bits) + rows) * (1 << slot_bits) + ids
    code_up = upright(code)
    lane = lax.broadcasted_iota(i32, (slots, 128), 1)

    def shifted(x, bits):
        return lax.shift_right_logical(x, jnp.full_like(x, bits))

    for k in range(n):
        hit = (rank == lane + k * quota) & (lane < quota)
        found = jnp.sum(jnp.where(hit, code_up, 0), axis=0, keepdims=True)
        plan[k, 0:1, :] = shifted(found, slot_bits + row_bits + 1)
        plan[k, 1:2, :] = found & ((1 << slot_bits) - 1)
        plan[k, 2:3, :] = shifted(found, slot_bits) & ((1 << row_bits) - 1)
        plan[k, 3:4, :] = shifted(found, slot_bits + row_bits) & 1
        plan[k, 4:8, :] = jnp.zeros((4, 128), i32)

    pl.semaphore_wait(barrier, n)

    def req_copy(d):
        dst = lax.rem(me + d, n)
        return pltpu.make_async_remote_copy(
            src_ref=plan.at[dst],
            dst_ref=asked.at[me],
            send_sem=req_send.at[d],
            recv_sem=req_recv.at[d],
            device_id={"sample": dst},
            device_id_type=MESH,
        )

    def coef_copy(h, d):
        dst = lax.rem(me + d, n)
        return pltpu.make_async_remote_copy(
            src_ref=send.at[h, dst],
            dst_ref=recv.at[h, me],
            send_sem=c_send.at[h, d],
            recv_sem=c_recv.at[h, d],
            device_id={"sample": dst},
            device_id_type=MESH,
        )

    def grad_copy(h, d):
        dst = lax.rem(me + d, n)
        return pltpu.make_async_remote_copy(
            src_ref=gsend.at[h, dst],
            dst_ref=grad_ref.at[h, me],
            send_sem=g_send.at[h, d],
            recv_sem=g_recv.at[h, d],
            device_id={"sample": dst},
            device_id_type=MESH,
        )

    def swap_copy(h):
        return pltpu.make_async_remote_copy(
            src_ref=marg.at[h],
            dst_ref=marg_other.at[h],
            send_sem=m_send.at[h],
            recv_sem=m_recv.at[h],
            device_id={"feature": other},
            device_id_type=MESH,
        )

    for i in range(n - 1):
        req_copy(_distance(n, i)).start()

    bring_mine = pltpu.make_async_copy(plan, mine, want_sem.at[0])
    bring_mine.start()
    for h in range(PARTS):
        for b in range(share):
            at = slice(b * width, (b + 1) * width)
            blocks[h, b] = coef_ref[h * reps : (h + 1) * reps, at].astype(BF16)
    asked[me] = plan[me]
    bring_mine.wait()

    def pack(h, table, target, slot):
        def some(g, carry):
            for u in range(step):
                j = g * step + u
                target[h, slot, j] = blocks[h, table[slot, 0, j]]
            return carry

        lax.fori_loop(0, quota // step, some, 0)

    def serve(i, carry):
        up = _distance(n, i)
        src = lax.rem(me + up, n)
        req_copy(n - up).wait_recv()
        bring = pltpu.make_async_copy(asked.at[src], wanted.at[src], want_sem.at[1])
        bring.start()
        bring.wait()
        pack(0, wanted, send, src)
        coef_copy(0, up).start()
        return carry

    lax.fori_loop(0, n - 1, serve, 0)
    keep_asked = pltpu.make_async_copy(asked, asked_out, asked_sem)
    keep_asked.start()

    def prepare(i, carry):
        pack(1, wanted, send, lax.rem(me + i, n))
        return carry

    lax.fori_loop(1, n, prepare, 0)
    for h in range(PARTS):
        pack(h, mine, recv, me)

    key = jnp.where(live > 0, rows, row_blocks)
    key_up = upright(key)
    ahead = jnp.where((key < key_up) | ((key == key_up) & (jj < ii)), 1, 0)
    row_rank = jnp.sum(ahead, axis=1, keepdims=True)

    def by_row(shift, column):
        return jnp.sum(jnp.where(row_rank + shift == jj, column, 0), axis=0, keepdims=True)

    sums[...] = jnp.zeros_like(sums)
    sums[0:1, 0:slots] = by_row(0, rank)
    sums[1:2, 0:slots] = jnp.where(by_row(0, key_up) == by_row(1, key_up), 1, 0)
    upto = jnp.sum(jnp.where(key_up <= lane, 1, 0), axis=0, keepdims=True)
    here = jnp.sum(jnp.where(key_up == lane, 1, 0), axis=0, keepdims=True)
    sums[2:3, 0:128] = jnp.maximum(upto - 1, 0)
    sums[3:4, 0:128] = jnp.minimum(here, 1)
    bring_sums = pltpu.make_async_copy(sums, meta, want_sem.at[0])
    bring_sums.start()
    bring_sums.wait()
    load_values.wait()

    def forward(h, src):
        def some(g, carry):
            for u in range(step):
                j = g * step + u
                prod[src * quota + j] = lax.dot_general(
                    recv[h, src, j],
                    vbuf[mine[src, 1, j]],
                    (((1,), (1,)), ((), ())),
                    preferred_element_type=F32,
                )
            return carry

        lax.fori_loop(0, quota // step, some, 0)

    def row_sums(h):
        def one(g, acc):
            for u in range(step):
                q = g * step + u
                acc = acc * meta[1, q].astype(F32) + prod[meta[0, q]]
                run[q] = acc
            return acc

        lax.fori_loop(0, slots // step, one, jnp.zeros((reps, width), F32))

        def take(r, carry):
            marg[h, r] = run[meta[2, r]] * meta[3, r].astype(F32)
            return carry

        lax.fori_loop(0, row_blocks, take, 0)

    def residuals(h):
        def one(r, carry):
            m = marg[h, r] + marg_other[h, r]
            at = pl.ds(pl.multiple_of(r * width, width), width)
            c = counts_ref[h * reps : (h + 1) * reps, at].astype(F32)
            y = labels_ref[r].astype(F32)
            resid[h, r] = (c * (jax.nn.sigmoid(m) - y)).astype(BF16)
            return carry

        lax.fori_loop(0, row_blocks, one, 0)

    def backward(h, dst):
        def some(g, carry):
            for u in range(step):
                j = g * step + u
                back = lax.dot_general(
                    resid[h, mine[dst, 2, j]],
                    vbuf[mine[dst, 1, j]],
                    (((1,), (0,)), ((), ())),
                    preferred_element_type=F32,
                )
                gsend[h, dst, j] = (back * mine[dst, 3, j].astype(F32)).astype(BF16)
            return carry

        lax.fori_loop(0, quota // step, some, 0)

    def own_copy(h):
        return pltpu.make_async_copy(gsend.at[h, me], grad_ref.at[h, me], own_sem.at[h])

    forward(0, me)

    def arrive_first(i, carry):
        d = _distance(n, i)
        coef_copy(0, d).wait_send()
        coef_copy(1, d).start()
        coef_copy(0, d).wait_recv()
        forward(0, lax.rem(me + n - d, n))
        return carry

    lax.fori_loop(0, n - 1, arrive_first, 0)
    row_sums(0)
    swap_copy(0).start()
    forward(1, me)
    swap_copy(0).wait()
    residuals(0)

    def give_first(i, carry):
        d = _distance(n, i)
        backward(0, lax.rem(me + d, n))
        coef_copy(1, d).wait_send()
        grad_copy(0, d).start()
        return carry

    lax.fori_loop(0, n - 1, give_first, 0)
    backward(0, me)
    own_copy(0).start()

    def arrive_second(i, carry):
        d = _distance(n, i)
        coef_copy(1, d).wait_recv()
        forward(1, lax.rem(me + n - d, n))
        return carry

    lax.fori_loop(0, n - 1, arrive_second, 0)
    row_sums(1)
    swap_copy(1).start()
    swap_copy(1).wait()
    residuals(1)

    def give_second(i, carry):
        d = _distance(n, i)
        backward(1, lax.rem(me + d, n))
        grad_copy(1, d).start()
        return carry

    lax.fori_loop(0, n - 1, give_second, 0)
    backward(1, me)
    own_copy(1).start()

    def finish(i, carry):
        d = _distance(n, i)
        req_copy(d).wait_send()
        for h in range(PARTS):
            grad_copy(h, d).wait_send()
            grad_copy(h, d).wait_recv()
        return carry

    lax.fori_loop(0, n - 1, finish, 0)
    keep_asked.wait()
    for h in range(PARTS):
        own_copy(h).wait()


def add_kernel(n, quota, step, scale, asked_ref, grad_ref, out_ref, gbuf, asked, sems, asked_sem):
    reps, width = gbuf.shape[3:]

    def fetch(h, s):
        return pltpu.make_async_copy(grad_ref.at[h, s], gbuf.at[h, s], sems.at[h, s])

    bring = pltpu.make_async_copy(asked_ref, asked, asked_sem)
    bring.start()
    for s in range(n):
        for h in range(PARTS):
            fetch(h, s).start()
    out_ref[...] = jnp.zeros_like(out_ref)
    bring.wait()

    def source(s, carry):
        for h in range(PARTS):
            fetch(h, s).wait()

        def some(g, inner):
            for u in range(step):
                j = g * step + u
                at = pl.ds(pl.multiple_of(asked[s, 0, j] * width, width), width)
                for h in range(PARTS):
                    out_ref[h * reps : (h + 1) * reps, at] += gbuf[h, s, j].astype(F32) * scale
            return inner

        return lax.fori_loop(0, quota // step, some, carry)

    lax.fori_loop(0, n, source, 0)


def local(blk_values, blk_rows, blk_cols, blk_count, boot_counts, labels, coefs):
    values = blk_values[0, 0]
    slots, width = values.shape[0], values.shape[1]
    reps = coefs.shape[1] // PARTS
    n = lax.axis_size("sample")
    row_blocks = boot_counts.shape[0] // width
    share = coefs.shape[0] // width
    quota, step = _sizes(n, slots)
    wide = -(-slots // 128) * 128
    vmem = pl.BlockSpec(memory_space=pltpu.VMEM)
    smem = pl.BlockSpec(memory_space=pltpu.SMEM)
    hbm = pl.BlockSpec(memory_space=pl.ANY)
    dma = pltpu.SemaphoreType.DMA
    per_owner = (PARTS, n, quota, reps, width)
    per_row = (PARTS, row_blocks, reps, width)
    asked, grads = pl.pallas_call(
        functools.partial(exchange_kernel, n, quota, step, row_blocks),
        out_shape=[
            jax.ShapeDtypeStruct((n, 8, 128), jnp.int32),
            jax.ShapeDtypeStruct(per_owner, BF16),
        ],
        in_specs=[smem, vmem, vmem, vmem, vmem, vmem, hbm],
        out_specs=[hbm, hbm],
        scratch_shapes=[
            pltpu.VMEM((slots, width, width), BF16),
            pltpu.VMEM((PARTS, share, reps, width), BF16),
            pltpu.VMEM(per_owner, BF16),
            pltpu.VMEM(per_owner, BF16),
            pltpu.VMEM((slots, reps, width), F32),
            pltpu.VMEM((slots, reps, width), F32),
            pltpu.VMEM(per_row, F32),
            pltpu.VMEM(per_row, F32),
            pltpu.VMEM(per_row, BF16),
            pltpu.VMEM(per_owner, BF16),
            pltpu.VMEM((n, 8, 128), jnp.int32),
            pltpu.VMEM((n, 8, 128), jnp.int32),
            pltpu.VMEM((8, wide), jnp.int32),
            pltpu.SMEM((n, 8, 128), jnp.int32),
            pltpu.SMEM((n, 8, 128), jnp.int32),
            pltpu.SMEM((8, wide), jnp.int32),
            dma,
            dma((n,)),
            dma((n,)),
            dma((2,)),
            dma,
            dma((PARTS, n)),
            dma((PARTS, n)),
            dma((PARTS,)),
            dma((PARTS,)),
            dma((PARTS, n)),
            dma((PARTS, n)),
            dma((PARTS,)),
        ],
        compiler_params=pltpu.CompilerParams(
            collective_id=0, has_side_effects=True, vmem_limit_bytes=56 * 2**20
        ),
        name="exchange",
    )(
        blk_count,
        blk_rows[0],
        blk_cols[0],
        coefs.T,
        boot_counts.T,
        labels.reshape(row_blocks, 1, width),
        values,
    )
    total = pl.pallas_call(
        functools.partial(add_kernel, n, quota, step, 1.0 / 16.0),
        out_shape=jax.ShapeDtypeStruct((PARTS * reps, coefs.shape[0]), F32),
        in_specs=[hbm, hbm],
        out_specs=vmem,
        scratch_shapes=[
            pltpu.VMEM(per_owner, BF16),
            pltpu.SMEM((n, 8, 128), jnp.int32),
            dma((PARTS, n)),
            dma,
        ],
        compiler_params=pltpu.CompilerParams(vmem_limit_bytes=56 * 2**20),
        name="add",
    )(asked, grads)
    return total.T


def solution(mesh):
    return jax.shard_map(
        local,
        mesh=mesh,
        in_specs=(
            P(("groups", "sample"), "feature", None, None, None),
            P(("groups", "sample"), "feature", None),
            P(("groups", "sample"), "feature", None),
            P(("groups", "sample"), "feature"),
            P(("groups", "sample"), None),
            P(("groups", "sample")),
            P(("groups", "feature", "sample"), None),
        ),
        out_specs=P(("groups", "feature", "sample"), None),
        check_vma=False,
    )
```

```python
import functools

import jax
import jax.numpy as jnp
from jax import lax
from jax.experimental import pallas as pl
from jax.experimental.pallas import tpu as pltpu
from jax.sharding import PartitionSpec as P

MESH = pl.DeviceIdType.MESH
F32 = jnp.float32
BF16 = jnp.bfloat16


PARTS = 2


def _sizes(n, slots):
    quota = slots // n
    step = max(u for u in range(1, 11) if quota % u == 0)
    return quota, step


def _distance(n, i):
    half = (i + 1) // 2
    return n // 2 + (1 - 2 * (i % 2)) * half


def _bits(size):
    return (size - 1).bit_length()


def exchange_kernel(
    n,
    quota,
    step,
    row_blocks,
    count_ref,
    rows_ref,
    cols_ref,
    labels_ref,
    coef_hbm,
    counts_hbm,
    values_ref,
    asked_out,
    grad_ref,
    coef_ref,
    counts_ref,
    vbuf,
    blocks,
    send,
    recv,
    prod,
    run,
    marg,
    marg_other,
    resid,
    gsend,
    plan,
    asked,
    sums,
    wanted,
    mine,
    meta,
    v_sem,
    req_send,
    req_recv,
    want_sem,
    asked_sem,
    c_send,
    c_recv,
    m_send,
    m_recv,
    g_send,
    g_recv,
    own_sem,
):
    me = lax.axis_index("sample")
    feat = lax.axis_index("feature")
    other = 1 - feat
    share, reps, width = blocks.shape[1:]
    slots = n * quota
    i32 = jnp.int32

    load_coefs = pltpu.make_async_copy(coef_hbm, coef_ref, v_sem.at[0])
    load_coefs.start()
    load_counts = pltpu.make_async_copy(counts_hbm, counts_ref, v_sem.at[1])
    load_values = pltpu.make_async_copy(values_ref, vbuf, v_sem.at[2])

    barrier = pltpu.get_barrier_semaphore()
    for d in range(1, n):
        pl.semaphore_signal(
            barrier, inc=1, device_id={"sample": lax.rem(me + d, n)}, device_id_type=MESH
        )
    pl.semaphore_signal(barrier, inc=1, device_id={"feature": other}, device_id_type=MESH)

    ii = lax.broadcasted_iota(i32, (slots, slots), 0)
    jj = lax.broadcasted_iota(i32, (slots, slots), 1)

    def upright(row):
        return jnp.sum(jnp.where(ii == jj, row, 0), axis=1, keepdims=True)

    share_bits, row_bits, slot_bits = _bits(share), _bits(row_blocks), _bits(slots)
    cols = cols_ref[...]
    rows = rows_ref[...]
    ids = lax.broadcasted_iota(i32, (1, slots), 1)
    live = (ids < count_ref[0, 0]).astype(i32)
    owner = lax.shift_right_logical(cols, jnp.full_like(cols, share_bits))
    owner_up = upright(owner)
    same = jnp.where((owner_up == owner) & (jj < ii), 1, 0)
    rank = owner_up * quota + jnp.sum(same, axis=1, keepdims=True)
    code = (cols & (share - 1)) * 2 + live
    code = (code * (1 << row_bits) + rows) * (1 << slot_bits) + ids
    code_up = upright(code)
    lane = lax.broadcasted_iota(i32, (slots, 128), 1)

    def shifted(x, bits):
        return lax.shift_right_logical(x, jnp.full_like(x, bits))

    for k in range(n):
        hit = (rank == lane + k * quota) & (lane < quota)
        found = jnp.sum(jnp.where(hit, code_up, 0), axis=0, keepdims=True)
        plan[k, 0:1, :] = shifted(found, slot_bits + row_bits + 1)
        plan[k, 1:2, :] = found & ((1 << slot_bits) - 1)
        plan[k, 2:3, :] = shifted(found, slot_bits) & ((1 << row_bits) - 1)
        plan[k, 3:4, :] = shifted(found, slot_bits + row_bits) & 1
        plan[k, 4:8, :] = jnp.zeros((4, 128), i32)

    pl.semaphore_wait(barrier, n)

    def req_copy(d):
        dst = lax.rem(me + d, n)
        return pltpu.make_async_remote_copy(
            src_ref=plan.at[dst],
            dst_ref=asked.at[me],
            send_sem=req_send.at[d],
            recv_sem=req_recv.at[d],
            device_id={"sample": dst},
            device_id_type=MESH,
        )

    def coef_copy(h, d):
        dst = lax.rem(me + d, n)
        return pltpu.make_async_remote_copy(
            src_ref=send.at[h, dst],
            dst_ref=recv.at[h, me],
            send_sem=c_send.at[h, d],
            recv_sem=c_recv.at[h, d],
            device_id={"sample": dst},
            device_id_type=MESH,
        )

    def grad_copy(h, d):
        dst = lax.rem(me + d, n)
        return pltpu.make_async_remote_copy(
            src_ref=gsend.at[h, dst],
            dst_ref=grad_ref.at[h, me],
            send_sem=g_send.at[h, d],
            recv_sem=g_recv.at[h, d],
            device_id={"sample": dst},
            device_id_type=MESH,
        )

    def swap_copy(h):
        return pltpu.make_async_remote_copy(
            src_ref=marg.at[h],
            dst_ref=marg_other.at[h],
            send_sem=m_send.at[h],
            recv_sem=m_recv.at[h],
            device_id={"feature": other},
            device_id_type=MESH,
        )

    for i in range(n - 1):
        req_copy(_distance(n, i)).start()

    bring_mine = pltpu.make_async_copy(plan, mine, want_sem.at[0])
    bring_mine.start()

    def round_blocks(h):
        for b in range(share):
            at = slice(b * width, (b + 1) * width)
            blocks[h, b] = coef_ref[h * reps : (h + 1) * reps, at].astype(BF16)

    asked[me] = plan[me]
    load_coefs.wait()
    load_values.start()
    load_counts.start()
    round_blocks(0)

    def pack(h, table, target, slot):
        def some(g, carry):
            for u in range(step):
                j = g * step + u
                target[h, slot, j] = blocks[h, table[slot, 0, j]]
            return carry

        lax.fori_loop(0, quota // step, some, 0)

    def hear(i, carry):
        req_copy(i).wait_recv()
        return carry

    lax.fori_loop(1, n, hear, 0)
    bring = pltpu.make_async_copy(asked, wanted, want_sem.at[1])
    bring.start()
    bring.wait()

    def serve(i, carry):
        up = _distance(n, i)
        pack(0, wanted, send, lax.rem(me + up, n))
        coef_copy(0, up).start()
        return carry

    lax.fori_loop(0, n - 1, serve, 0)
    round_blocks(1)
    bring_mine.wait()
    keep_asked = pltpu.make_async_copy(asked, asked_out, asked_sem)
    keep_asked.start()

    def prepare(i, carry):
        pack(1, wanted, send, lax.rem(me + i, n))
        return carry

    lax.fori_loop(1, n, prepare, 0)
    for h in range(PARTS):
        pack(h, mine, recv, me)

    key = jnp.where(live > 0, rows, row_blocks)
    key_up = upright(key)
    ahead = jnp.where((key < key_up) | ((key == key_up) & (jj < ii)), 1, 0)
    row_rank = jnp.sum(ahead, axis=1, keepdims=True)

    def by_row(shift, column):
        return jnp.sum(jnp.where(row_rank + shift == jj, column, 0), axis=0, keepdims=True)

    sums[...] = jnp.zeros_like(sums)
    sums[0:1, 0:slots] = by_row(0, rank)
    sums[1:2, 0:slots] = jnp.where(by_row(0, key_up) == by_row(1, key_up), 1, 0)
    upto = jnp.sum(jnp.where(key_up <= lane, 1, 0), axis=0, keepdims=True)
    here = jnp.sum(jnp.where(key_up == lane, 1, 0), axis=0, keepdims=True)
    sums[2:3, 0:128] = jnp.maximum(upto - 1, 0)
    sums[3:4, 0:128] = jnp.minimum(here, 1)
    bring_sums = pltpu.make_async_copy(sums, meta, want_sem.at[0])
    bring_sums.start()
    bring_sums.wait()
    load_values.wait()
    load_counts.wait()

    def forward(h, src):
        def some(g, carry):
            for u in range(step):
                j = g * step + u
                prod[src * quota + j] = lax.dot_general(
                    recv[h, src, j],
                    vbuf[mine[src, 1, j]],
                    (((1,), (1,)), ((), ())),
                    preferred_element_type=F32,
                )
            return carry

        lax.fori_loop(0, quota // step, some, 0)

    def row_sums(h):
        def one(g, acc):
            for u in range(step):
                q = g * step + u
                acc = acc * meta[1, q].astype(F32) + prod[meta[0, q]]
                run[q] = acc
            return acc

        lax.fori_loop(0, slots // step, one, jnp.zeros((reps, width), F32))

        def take(r, carry):
            marg[h, r] = run[meta[2, r]] * meta[3, r].astype(F32)
            return carry

        lax.fori_loop(0, row_blocks, take, 0)

    def residuals(h):
        def one(r, carry):
            m = marg[h, r] + marg_other[h, r]
            at = pl.ds(pl.multiple_of(r * width, width), width)
            c = counts_ref[h * reps : (h + 1) * reps, at].astype(F32)
            y = labels_ref[r].astype(F32)
            resid[h, r] = (c * (jax.nn.sigmoid(m) - y)).astype(BF16)
            return carry

        lax.fori_loop(0, row_blocks, one, 0)

    def backward(h, dst):
        def some(g, carry):
            for u in range(step):
                j = g * step + u
                back = lax.dot_general(
                    resid[h, mine[dst, 2, j]],
                    vbuf[mine[dst, 1, j]],
                    (((1,), (0,)), ((), ())),
                    preferred_element_type=F32,
                )
                gsend[h, dst, j] = (back * mine[dst, 3, j].astype(F32)).astype(BF16)
            return carry

        lax.fori_loop(0, quota // step, some, 0)

    def own_copy(h):
        return pltpu.make_async_copy(gsend.at[h, me], grad_ref.at[h, me], own_sem.at[h])

    forward(0, me)

    def arrive_first(i, carry):
        d = _distance(n, i)
        coef_copy(0, d).wait_send()
        coef_copy(1, d).start()
        coef_copy(0, d).wait_recv()
        forward(0, lax.rem(me + n - d, n))
        return carry

    lax.fori_loop(0, n - 1, arrive_first, 0)
    row_sums(0)
    swap_copy(0).start()
    forward(1, me)
    swap_copy(0).wait()
    residuals(0)

    def give_first(i, carry):
        d = _distance(n, i)
        backward(0, lax.rem(me + d, n))
        coef_copy(1, d).wait_send()
        grad_copy(0, d).start()
        return carry

    lax.fori_loop(0, n - 1, give_first, 0)
    backward(0, me)
    own_copy(0).start()

    def arrive_second(i, carry):
        d = _distance(n, i)
        coef_copy(1, d).wait_recv()
        forward(1, lax.rem(me + n - d, n))
        return carry

    lax.fori_loop(0, n - 1, arrive_second, 0)
    row_sums(1)
    swap_copy(1).start()
    swap_copy(1).wait()
    residuals(1)

    def give_second(i, carry):
        d = _distance(n, i)
        backward(1, lax.rem(me + d, n))
        grad_copy(1, d).start()
        return carry

    lax.fori_loop(0, n - 1, give_second, 0)
    backward(1, me)
    own_copy(1).start()

    def finish(i, carry):
        d = _distance(n, i)
        req_copy(d).wait_send()
        for h in range(PARTS):
            grad_copy(h, d).wait_send()
            grad_copy(h, d).wait_recv()
        return carry

    lax.fori_loop(0, n - 1, finish, 0)
    keep_asked.wait()
    for h in range(PARTS):
        own_copy(h).wait()


def add_kernel(n, quota, step, scale, asked_ref, grad_ref, out_ref, low, high, gbuf, asked, sems, asked_sem, out_sem):
    reps, width = gbuf.shape[3:]

    def fetch(h, s):
        return pltpu.make_async_copy(grad_ref.at[h, s], gbuf.at[h, s], sems.at[h, s])

    bring = pltpu.make_async_copy(asked_ref, asked, asked_sem)
    bring.start()
    for s in range(n):
        for h in range(PARTS):
            fetch(h, s).start()
    totals = (low, high)
    for total in totals:
        total[...] = jnp.zeros_like(total)
    bring.wait()

    def source(s, carry):
        for h in range(PARTS):
            fetch(h, s).wait()

        def some(g, inner):
            for u in range(step):
                j = g * step + u
                at = pl.ds(pl.multiple_of(asked[s, 0, j] * width, width), width)
                for h in range(PARTS):
                    totals[h][:, at] += gbuf[h, s, j].astype(F32) * scale
            return inner

        return lax.fori_loop(0, quota // step, some, carry)

    lax.fori_loop(0, n, source, 0)
    stores = [
        pltpu.make_async_copy(
            totals[h], out_ref.at[pl.ds(h * reps, reps)], out_sem.at[h]
        )
        for h in range(PARTS)
    ]
    for store in stores:
        store.start()
    for store in stores:
        store.wait()


def local(blk_values, blk_rows, blk_cols, blk_count, boot_counts, labels, coefs):
    values = blk_values[0, 0]
    slots, width = values.shape[0], values.shape[1]
    reps = coefs.shape[1] // PARTS
    n = lax.axis_size("sample")
    row_blocks = boot_counts.shape[0] // width
    share = coefs.shape[0] // width
    quota, step = _sizes(n, slots)
    wide = -(-slots // 128) * 128
    vmem = pl.BlockSpec(memory_space=pltpu.VMEM)
    smem = pl.BlockSpec(memory_space=pltpu.SMEM)
    hbm = pl.BlockSpec(memory_space=pl.ANY)
    dma = pltpu.SemaphoreType.DMA
    per_owner = (PARTS, n, quota, reps, width)
    per_row = (PARTS, row_blocks, reps, width)
    asked, grads = pl.pallas_call(
        functools.partial(exchange_kernel, n, quota, step, row_blocks),
        out_shape=[
            jax.ShapeDtypeStruct((n, 8, 128), jnp.int32),
            jax.ShapeDtypeStruct(per_owner, BF16),
        ],
        in_specs=[smem, vmem, vmem, vmem, hbm, hbm, hbm],
        out_specs=[hbm, hbm],
        scratch_shapes=[
            pltpu.VMEM((PARTS * reps, coefs.shape[0]), F32),
            pltpu.VMEM((PARTS * reps, boot_counts.shape[0]), jnp.int32),
            pltpu.VMEM((slots, width, width), BF16),
            pltpu.VMEM((PARTS, share, reps, width), BF16),
            pltpu.VMEM(per_owner, BF16),
            pltpu.VMEM(per_owner, BF16),
            pltpu.VMEM((slots, reps, width), F32),
            pltpu.VMEM((slots, reps, width), F32),
            pltpu.VMEM(per_row, F32),
            pltpu.VMEM(per_row, F32),
            pltpu.VMEM(per_row, BF16),
            pltpu.VMEM(per_owner, BF16),
            pltpu.VMEM((n, 8, 128), jnp.int32),
            pltpu.VMEM((n, 8, 128), jnp.int32),
            pltpu.VMEM((8, wide), jnp.int32),
            pltpu.SMEM((n, 8, 128), jnp.int32),
            pltpu.SMEM((n, 8, 128), jnp.int32),
            pltpu.SMEM((8, wide), jnp.int32),
            dma((3,)),
            dma((n,)),
            dma((n,)),
            dma((2,)),
            dma,
            dma((PARTS, n)),
            dma((PARTS, n)),
            dma((PARTS,)),
            dma((PARTS,)),
            dma((PARTS, n)),
            dma((PARTS, n)),
            dma((PARTS,)),
        ],
        compiler_params=pltpu.CompilerParams(
            collective_id=0, has_side_effects=True, vmem_limit_bytes=56 * 2**20
        ),
        name="exchange",
    )(
        blk_count,
        blk_rows[0],
        blk_cols[0],
        labels.reshape(row_blocks, 1, width),
        coefs.T,
        boot_counts.T,
        values,
    )
    total = pl.pallas_call(
        functools.partial(add_kernel, n, quota, step, 1.0 / 16.0),
        out_shape=jax.ShapeDtypeStruct((PARTS * reps, coefs.shape[0]), F32),
        in_specs=[hbm, hbm],
        out_specs=hbm,
        scratch_shapes=[
            pltpu.VMEM((reps, coefs.shape[0]), F32),
            pltpu.VMEM((reps, coefs.shape[0]), F32),
            pltpu.VMEM(per_owner, BF16),
            pltpu.SMEM((n, 8, 128), jnp.int32),
            dma((PARTS, n)),
            dma,
            dma((PARTS,)),
        ],
        compiler_params=pltpu.CompilerParams(vmem_limit_bytes=56 * 2**20),
        name="add",
    )(asked, grads)
    return total.T


def solution(mesh):
    return jax.shard_map(
        local,
        mesh=mesh,
        in_specs=(
            P(("groups", "sample"), "feature", None, None, None),
            P(("groups", "sample"), "feature", None),
            P(("groups", "sample"), "feature", None),
            P(("groups", "sample"), "feature"),
            P(("groups", "sample"), None),
            P(("groups", "sample")),
            P(("groups", "feature", "sample"), None),
        ),
        out_specs=P(("groups", "feature", "sample"), None),
        check_vma=False,
    )
```
